128 devices in a mesh: node: 32 (over y, z, core), local: 4 (over x).
Axes of the slice: x: 4, y: 4, z: 4, core: 2. Of those that a mesh axis runs over, the one named last changes fastest.
Arguments:
- layer_input: bfloat16 [2048, 3584], P(('node', 'local')), may hold values from -6 to 6
- grad_output: bfloat16 [2048, 3584], P(('node', 'local')), may hold values from -6 to 6
- expert_ids: int32 [2048, 8], P(('node', 'local')), may hold values from 0 to 127, as said below
- route_weights: bfloat16 [2048, 8], P(('node', 'local')), may hold values from 0.099609375 to 1
- w_gate: bfloat16 [128, 3584, 1024], P(('node', 'local')), may hold values from -0.09375 to 0.09375
- w_up: bfloat16 [128, 3584, 1024], P(('node', 'local')), may hold values from -0.09375 to 0.09375
- w_down: bfloat16 [128, 1024, 3584], P(('node', 'local')), may hold values from -0.1875 to 0.1875
Outputs:
- input_grad: bfloat16 [2048, 3584], P(('node', 'local'))
The draws below stay inside these ranges and needn't reach their ends.
Inputs may be any that keep to these rules, and one draw needn't show every extreme that they name: `expert_ids`: each row names 8 different experts, two in each of four different node groups, where expert e lies in node group e // 4 and is held by device e. Among the 16 tokens of one device at most 4 name a given node group, and in every device some group is named by exactly 4 of them; at most 2 name a given expert, and every device has an expert named exactly 2 times. Every expert is named by exactly 32 tokens of the devices of each local index, so by 128 tokens in all.
All inputs are finite; a program needn't handle non-finite values.
Results may differ from the reference program's by a relative error of at most 0.0049.
Values may be sent and summed in bfloat16 or wider, within the bound.
A program may use at most 128 MiB of HBM per device.

```python
import math
import jax
import jax.numpy as jnp
from jax import lax

D = 3584
HW = 1024
TOPK = 8
TOK_DEV = 16
EXPERTS = 128
TOKENS = 2048
MOSTG = 4
EXPERT_ROWS = 128
N_NODE = 32
N_LOCAL = 4


def route_table(key):
    devices = N_NODE * N_LOCAL
    half_most = MOSTG // 2
    base_units = TOK_DEV // N_NODE
    extra_units = 2 * TOK_DEV - base_units * N_NODE
    headroom = half_most - base_units
    steps_idx = jnp.arange(N_NODE, dtype=jnp.int32)
    profile = (base_units + jnp.clip(extra_units - steps_idx * headroom, 0, headroom)).astype(jnp.int32)
    shares = jnp.stack([jax.random.permutation(jax.random.fold_in(key, 100 + local_idx), profile) for local_idx in range(N_LOCAL)])
    offsets = jnp.stack([jax.random.permutation(jax.random.fold_in(key, 200 + local_idx), N_NODE) for local_idx in range(N_LOCAL)]).astype(jnp.int32)
    device_ids = jnp.arange(devices, dtype=jnp.int32)
    node_of = device_ids // N_LOCAL
    lane_of = device_ids % N_LOCAL
    rotated = (steps_idx[None, :] - offsets[lane_of, node_of][:, None]) % N_NODE
    units = shares[lane_of[:, None], rotated]
    counts = 2 * units
    ends = jnp.cumsum(counts, axis=1)
    starts = ends - counts
    positions = jnp.arange(4 * TOK_DEV, dtype=jnp.int32)
    group_at = jnp.sum((positions[None, :, None] >= ends[:, None, :]).astype(jnp.int32), axis=2)
    rank_in = positions[None, :] - jnp.take_along_axis(starts, group_at, axis=1)
    unit_at = jnp.take_along_axis(units, group_at, axis=1)
    half_at = rank_in // jnp.maximum(unit_at, 1)
    scores = jax.random.randint(jax.random.fold_in(key, 300), (devices, N_NODE, 4), 0, 1 << 20) * 4 + jnp.arange(4, dtype=jnp.int32)
    lane_perm = jnp.argsort(scores, axis=2).astype(jnp.int32)
    perm_at = lane_perm[device_ids[:, None], group_at]
    first_lane = jnp.take_along_axis(perm_at, half_at[..., None], axis=2)[..., 0]
    second_lane = jnp.take_along_axis(perm_at, half_at[..., None] + 2, axis=2)[..., 0]
    pairs = jnp.stack([group_at * 4 + first_lane, group_at * 4 + second_lane], axis=2)
    per_token = pairs.reshape(devices, 4, TOK_DEV, 2).transpose(0, 2, 1, 3).reshape(devices, TOK_DEV, 8)
    token_scores = jax.random.randint(jax.random.fold_in(key, 400), (devices, TOK_DEV), 0, 1 << 20) * TOK_DEV + jnp.arange(TOK_DEV, dtype=jnp.int32)
    token_perm = jnp.argsort(token_scores, axis=1).astype(jnp.int32)
    per_token = jnp.take_along_axis(per_token, token_perm[..., None], axis=1)
    column_scores = jax.random.randint(jax.random.fold_in(key, 500), (devices, TOK_DEV, 8), 0, 1 << 20) * 8 + jnp.arange(8, dtype=jnp.int32)
    column_perm = jnp.argsort(column_scores, axis=2).astype(jnp.int32)
    per_token = jnp.take_along_axis(per_token, column_perm, axis=2)
    return per_token.reshape(devices * TOK_DEV, 8).astype(jnp.int32)


def draw_expert_ids(key, part):
    key = jax.random.fold_in(key, 11)
    return route_table(key)


def levels(rng, dims, pieces, low, high):
    def one(axis_at, parts):
        draws = jax.random.uniform(jax.random.fold_in(jax.random.fold_in(rng, 6), axis_at), (parts,), jnp.float32, low / len(pieces), high / len(pieces))
        return jnp.repeat(jnp.exp(draws), dims[axis_at] // parts).reshape((-1,) + (1,) * (len(dims) - axis_at - 1))

    factor_of = one(*pieces[0])
    for cut in pieces[1:]:
        factor_of = factor_of * one(*cut)
    return factor_of


def gaussian(rng, shape, scale, most, shards=(), held_as=jnp.bfloat16):
    array = jax.random.normal(rng, shape, jnp.float32) * scale
    if len(shards) > 0:
        array = levels(rng, shape, shards, -0.22, 0.18) * array
    return jnp.clip(array, min=-most, max=most).astype(held_as)


def setup_inputs(seed: int = 0) -> dict:
    splits = jax.random.split(jax.random.key(seed), 8)
    layer_input = gaussian(splits[0], (TOKENS, D), 1.0, 6.0, ((0, 128),))
    grad_output = gaussian(splits[1], (TOKENS, D), 1.0, 6.0, ((0, 128),))
    expert_ids = draw_expert_ids(jax.random.fold_in(splits[7], 71), 0)
    route_weights = jnp.clip(jnp.exp(math.log(1.0) - 2.306499 * jax.random.uniform(splits[3], (TOKENS, TOPK), jnp.float32) ** levels(splits[3], (TOKENS, TOPK), ((0, 128),), -0.2, 0.2)), 0.099609375, 1.0).astype(jnp.bfloat16)
    w_gate = gaussian(splits[4], (EXPERTS, D, HW), D ** -0.5, 0.09375, ((0, 128),))
    w_up = gaussian(splits[5], (EXPERTS, D, HW), D ** -0.5, 0.09375, ((0, 128),))
    w_down = gaussian(splits[6], (EXPERTS, HW, D), HW ** -0.5, 0.1875, ((0, 128),))
    return {"layer_input": layer_input, "grad_output": grad_output, "expert_ids": expert_ids, "route_weights": route_weights, "w_gate": w_gate, "w_up": w_up, "w_down": w_down}


def expert_grad(packed_rows, scales, w_gate, w_up, w_down):
    in_width = w_gate.shape[0]
    inputs_part = packed_rows[:, :in_width]
    grads_part = packed_rows[:, in_width:]
    contract = (((1,), (1,)), ((), ()))
    pre_gate = jnp.dot(inputs_part, w_gate, preferred_element_type=jnp.float32)
    pre_up = jnp.dot(inputs_part, w_up, preferred_element_type=jnp.float32)
    hidden_grad = scales.astype(jnp.float32)[:, None] * lax.dot_general(grads_part, w_down, contract, preferred_element_type=jnp.float32)
    sigmoid_gate = jax.nn.sigmoid(pre_gate)
    d_gate = (hidden_grad * pre_up * sigmoid_gate * (1.0 + pre_gate * (1.0 - sigmoid_gate))).astype(jnp.bfloat16)
    d_up = (hidden_grad * pre_gate * sigmoid_gate).astype(jnp.bfloat16)
    return lax.dot_general(d_gate, w_gate, contract, preferred_element_type=jnp.float32) + lax.dot_general(d_up, w_up, contract, preferred_element_type=jnp.float32)

def reference(layer_input, grad_output, expert_ids, route_weights, w_gate, w_up, w_down):
    packed = jnp.concatenate([layer_input, grad_output], axis=1)
    tok_total = layer_input.shape[0]
    model_width = layer_input.shape[1]

    def one_expert(running, expert):
        matched = expert_ids == expert
        scales = lax.optimization_barrier(jnp.sum(jnp.where(matched, route_weights, jnp.zeros_like(route_weights)), axis=1))
        is_named = jnp.any(matched, axis=1)
        picked = jnp.nonzero(is_named, size=EXPERT_ROWS, fill_value=0)[0].astype(jnp.int32)
        grads_rows = expert_grad(packed[picked], scales[picked], w_gate[expert], w_up[expert], w_down[expert])
        return (running.at[picked].add(grads_rows), None)
    running = jnp.zeros((tok_total, model_width), jnp.float32)
    running, _ = lax.scan(one_expert, running, jnp.arange(EXPERTS, dtype=jnp.int32))
    return running.astype(jnp.bfloat16)
```

```python
import jax
import jax.numpy as jnp
from jax import lax
from jax.experimental import pallas as pl
from jax.experimental.pallas import tpu as pltpu
from jax.sharding import PartitionSpec as P

MESH = pl.DeviceIdType.MESH
BF16 = jnp.bfloat16
F32 = jnp.float32

D = 3584
HW = 1024
TOK = 16
OUT_CUTS = (768, 1024, 1024, 768)
BACK_CUTS = (1024, 1024, 768, 768)
NB = 256


def pieces(cuts):
    starts = [sum(cuts[:i]) for i in range(len(cuts))]
    return tuple(zip(starts, cuts))


OUT_PIECES = pieces(OUT_CUTS)
BACK_PIECES = pieces(BACK_CUTS)


def iota(shape, dim):
    return lax.broadcasted_iota(jnp.int32, shape, dim)


def dot(a, b):
    return jnp.dot(a, b, preferred_element_type=F32)


def dot_t(a, b):
    return lax.dot_general(a, b, (((1,), (1,)), ((), ())), preferred_element_type=F32)


def as01(mask):
    return jnp.where(mask, 1.0, 0.0).astype(BF16)


def rows(start, size):
    return pl.ds(pl.multiple_of(start, size), size)


def kernel(
    x_in,
    g_in,
    ids,
    route,
    wg_hbm,
    wu_hbm,
    wd_hbm,
    out,
    wg,
    wu,
    wd,
    w_tok,
    m1,
    m2,
    m_s,
    m_r,
    mx_s,
    mx_r,
    a1,
    a2,
    s1,
    s2,
    r1,
    r2,
    x_s,
    x_r,
    sel1,
    sel2,
    sel1t,
    sel2t,
    pick1,
    pick2,
    pick1t,
    pick2t,
    pre_gate,
    pre_up,
    hidden,
    d_gate,
    d_up,
    y_s,
    y_r,
    u_s,
    u_r,
    q_s,
    q_r,
    w_sem,
    meta_sem,
    h1_sem,
    h2_sem,
    x_sem,
    b1_sem,
    b2_sem,
    b3_sem,
    send_sem,
):
    node = lax.axis_index("node")
    xi = lax.axis_index("local")
    yi, zi, ci = node // 8, lax.rem(node // 2, 4), lax.rem(node, 2)

    def turn(v, k, size):
        return lax.rem(v + k, size)

    def device(y, z, c, x):
        return (y * 8 + z * 2 + c, x)

    far_first = (2, 1, 3)
    y_line = [(turn(yi, k, 4), device(turn(yi, k, 4), zi, ci, xi)) for k in far_first]
    z_line = [(turn(zi, k, 4), device(yi, turn(zi, k, 4), ci, xi)) for k in far_first]
    x_line = [(turn(xi, k, 4), device(yi, zi, ci, turn(xi, k, 4))) for k in far_first]
    steps = [(k, c) for k in far_first for c in (0, 1)] + [(0, 1)]
    zc_plane = [
        (turn(zi, k, 4) * 2 + turn(ci, c, 2), device(yi, turn(zi, k, 4), turn(ci, c, 2), xi))
        for k, c in steps
    ]
    yc_plane = [
        (turn(yi, k, 4) * 2 + turn(ci, c, 2), device(turn(yi, k, 4), zi, turn(ci, c, 2), xi))
        for k, c in steps
    ]
    lines = (y_line, z_line)
    planes = (zc_plane, yc_plane)
    line_at = (yi, zi)
    plane_at = (zi * 2 + ci, yi * 2 + ci)

    def local_copy(src, dst, sem):
        pltpu.make_async_copy(src, dst, sem).start()

    def remote_copy(src, dst, sem, send, target):
        pltpu.make_async_remote_copy(
            src_ref=src,
            dst_ref=dst,
            send_sem=send_sem.at[send],
            recv_sem=sem,
            device_id=target,
            device_id_type=MESH,
        ).start()

    def await_bytes(ref, sem):
        pltpu.make_async_copy(ref, ref, sem).wait()

    def weight_copies(i):
        start, width = OUT_PIECES[i]
        cut = pl.ds(start, width)
        return (
            pltpu.make_async_copy(wg_hbm.at[0, cut, :], wg.at[cut, :], w_sem.at[0, i]),
            pltpu.make_async_copy(wu_hbm.at[0, cut, :], wu.at[cut, :], w_sem.at[1, i]),
            pltpu.make_async_copy(wd_hbm.at[0, :, cut], wd.at[:, cut], w_sem.at[2, i]),
        )

    barrier = pltpu.get_barrier_semaphore()
    partners = [d for _, d in zc_plane] + [d for _, d in yc_plane[:-1]] + [d for _, d in x_line]
    for target in partners:
        pl.semaphore_signal(barrier, inc=1, device_id=target, device_id_type=MESH)

    lane = iota((TOK, 128), 1)
    table = jnp.zeros((TOK, 128), F32)
    id_block, route_block = ids[...], route[...].astype(F32)
    for k in range(8):
        table += jnp.where(id_block[:, k : k + 1] == lane, route_block[:, k : k + 1], 0.0)
    w_tok[...] = table.astype(BF16)

    pl.semaphore_wait(barrier, len(partners))

    metas = (m1, m2)
    gathered = (a1, a2)
    sources = (x_in, g_in)
    spread_s, spread_r = (s1, s2), (r1, r2)
    sel, sel_t = (sel1, sel2), (sel1t, sel2t)
    pick, pick_t = (pick1, pick2), (pick1t, pick2t)

    for p in (0, 1):
        mine = metas[p].at[rows(line_at[p] * TOK, TOK), :]
        for _, target in lines[p]:
            remote_copy(w_tok, mine, meta_sem.at[p], p, target)
        local_copy(w_tok, mine, meta_sem.at[p])

    def gather(i):
        start, width = OUT_PIECES[i]
        cut = pl.ds(start, width)
        for p in (0, 1):
            mine = gathered[p].at[rows(line_at[p] * TOK, TOK), cut]
            for _, target in lines[p]:
                remote_copy(sources[p].at[:, cut], mine, h1_sem.at[p, i], 4 + p, target)
            local_copy(sources[p].at[:, cut], mine, h1_sem.at[p, i])

    def spread(i):
        start, width = OUT_PIECES[i]
        cut = pl.ds(start, width)
        for p in (0, 1):
            await_bytes(gathered[p].at[:, cut], h1_sem.at[p, i])
            spread_s[p][:, cut] = dot(sel[p][...], gathered[p][:, cut]).astype(BF16)
            mine = rows(plane_at[p] * TOK, TOK)
            for at, target in planes[p]:
                remote_copy(
                    spread_s[p].at[rows(at * TOK, TOK), cut],
                    spread_r[p].at[mine, cut],
                    h2_sem.at[p, i],
                    6 + p,
                    target,
                )
            local_copy(spread_s[p].at[mine, cut], spread_r[p].at[mine, cut], h2_sem.at[p, i])

    def forward(i):
        start, width = OUT_PIECES[i]
        cut = pl.ds(start, width)
        for p in (0, 1):
            await_bytes(spread_r[p].at[:, cut], h2_sem.at[p, i])
            x_s[:, pl.ds(2 * start + p * width, width)] = dot(
                pick[p][...], spread_r[p][:, cut]
            ).astype(BF16)
        both = pl.ds(2 * start, 2 * width)
        mine = rows(xi * 32, 32)
        for at, target in x_line:
            remote_copy(x_s.at[rows(at * 32, 32), both], x_r.at[mine, both], x_sem.at[i], 8, target)
        local_copy(x_s.at[mine, both], x_r.at[mine, both], x_sem.at[i])

    def multiply(i):
        start, width = OUT_PIECES[i]
        cut = pl.ds(start, width)
        both = pl.ds(2 * start, 2 * width)
        for copy in weight_copies(i):
            copy.wait()
        await_bytes(x_r.at[:, both], x_sem.at[i])
        x_part = x_r[:, pl.ds(2 * start, width)]
        g_part = x_r[:, pl.ds(2 * start + width, width)]

        @pl.loop(0, HW // NB)
        def _(n):
            block = rows(n * NB, NB)
            gate = dot(x_part, wg[cut, block])
            up = dot(x_part, wu[cut, block])
            hid = dot_t(g_part, wd[block, cut])
            if i == 0:
                pre_gate[:, block] = gate
                pre_up[:, block] = up
                hidden[:, block] = hid
            else:
                pre_gate[:, block] += gate
                pre_up[:, block] += up
                hidden[:, block] += hid

    def choose_tokens():
        row, col = iota((128, 128), 0), iota((128, 128), 1)
        group = col >> 2
        named = (
            ((group >> 3) == yi) & ((group & 7) == (row >> 4)),
            (((group >> 1) & 3) == zi) & (((group >> 3) * 2 + (group & 1)) == (row >> 4)),
        )
        t0, t1 = iota((64, 64), 0), iota((64, 64), 1)
        same = (t0 >> 4) == (t1 >> 4)
        before, after = as01(same & (t0 < t1)), as01(same & (t1 < t0))
        r0, c0 = iota((128, 64), 0), iota((128, 64), 1)
        r1_, c1_ = iota((64, 128), 0), iota((64, 128), 1)
        for p in (0, 1):
            await_bytes(metas[p], meta_sem.at[p])
            hits = as01(metas[p][...].astype(F32) > 0)
            want = as01(named[p])
            hit = dot_t(want, hits) > 0.5
            rank = dot(as01(hit), before).astype(jnp.int32)
            ok = hit & (((r0 >> 2) & 3) == (c0 >> 4)) & ((r0 & 3) == rank)
            sel[p][...] = as01(ok)
            hit_t = dot_t(hits, want) > 0.5
            rank_t = dot(after, as01(hit_t)).astype(jnp.int32)
            ok_t = hit_t & (((c1_ >> 2) & 3) == (r1_ >> 4)) & ((c1_ & 3) == rank_t)
            sel_t[p][...] = as01(ok_t)
        m_s[...] = dot(sel1[...], m1[...]).astype(BF16)
        mine = rows(plane_at[0] * TOK, TOK)
        for at, target in planes[0]:
            remote_copy(m_s.at[rows(at * TOK, TOK), :], m_r.at[mine, :], meta_sem.at[2], 2, target)
        local_copy(m_s.at[mine, :], m_r.at[mine, :], meta_sem.at[2])

    def choose_slots():
        row, col = iota((128, 128), 0), iota((128, 128), 1)
        await_bytes(m_r, meta_sem.at[2])
        hits = as01(m_r[...].astype(F32) > 0)
        want = as01(col == node * 4 + (row >> 5))
        hit = dot_t(want, hits) > 0.5
        rank = dot(as01(hit), as01(row < col)).astype(jnp.int32)
        p1 = as01(hit & (rank == (row & 31)))
        pick1[...] = p1
        hit_t = dot_t(hits, want) > 0.5
        rank_t = dot(as01(col < row), as01(hit_t)).astype(jnp.int32)
        p1t = as01(hit_t & (rank_t == (col & 31)))
        pick1t[...] = p1t
        moved = ((row >> 2) & 3) * 32 + (row & 16) + (row >> 5) * 4 + (row & 3)
        swap = as01(moved == col)
        pick2[...] = dot(p1, swap).astype(BF16)
        pick2t[...] = dot(swap, p1t).astype(BF16)
        mx_s[...] = dot(p1, m_r[...]).astype(BF16)
        mine = rows(xi * 32, 32)
        for at, target in x_line:
            remote_copy(mx_s.at[rows(at * 32, 32), :], mx_r.at[mine, :], meta_sem.at[3], 3, target)
        local_copy(mx_s.at[mine, :], mx_r.at[mine, :], meta_sem.at[3])

    def activate():
        await_bytes(mx_r, meta_sem.at[3])
        scale = jnp.sum(
            jnp.where(iota((128, 128), 1) == node * 4 + xi, mx_r[...].astype(F32), 0.0),
            axis=1,
            keepdims=True,
        )

        @pl.loop(0, HW // NB)
        def _(n):
            block = rows(n * NB, NB)
            gate, up = pre_gate[:, block], pre_up[:, block]
            grad = scale * hidden[:, block]
            s = jax.nn.sigmoid(gate)
            d_gate[:, block] = (grad * up * s * (1.0 + gate * (1.0 - s))).astype(BF16)
            d_up[:, block] = (grad * gate * s).astype(BF16)

    def back_rows(i):
        start, width = BACK_PIECES[i]
        cut = pl.ds(start, width)

        @pl.loop(0, width // NB)
        def _(n):
            block = rows(start + n * NB, NB)
            total = dot_t(d_gate[...], wg[block, :]) + dot_t(d_up[...], wu[block, :])
            y_s[:, block] = total.astype(BF16)

        mine = rows(xi * 32, 32)
        for at, target in x_line:
            remote_copy(y_s.at[rows(at * 32, 32), cut], y_r.at[mine, cut], b1_sem.at[i], 9, target)
        local_copy(y_s.at[mine, cut], y_r.at[mine, cut], b1_sem.at[i])

    def back_slots(i):
        start, width = BACK_PIECES[i]
        cut = pl.ds(start, width)
        p = i % 2
        await_bytes(y_r.at[:, cut], b1_sem.at[i])
        u_s[:, cut] = dot(pick_t[p][...], y_r[:, cut]).astype(BF16)
        mine = rows(plane_at[p] * TOK, TOK)
        for at, target in planes[p]:
            remote_copy(
                u_s.at[rows(at * TOK, TOK), cut], u_r.at[mine, cut], b2_sem.at[i], 10, target
            )
        local_copy(u_s.at[mine, cut], u_r.at[mine, cut], b2_sem.at[i])

    def back_tokens(i):
        start, width = BACK_PIECES[i]
        cut = pl.ds(start, width)
        p = i % 2
        await_bytes(u_r.at[:, cut], b2_sem.at[i])
        q_s[:, cut] = dot(sel_t[p][...], u_r[:, cut]).astype(BF16)
        mine = rows(line_at[p] * TOK, TOK)
        for at, target in lines[p]:
            remote_copy(
                q_s.at[rows(at * TOK, TOK), cut], q_r.at[mine, cut], b3_sem.at[i], 11, target
            )
        local_copy(q_s.at[mine, cut], q_r.at[mine, cut], b3_sem.at[i])

    def finish(i):
        start, width = BACK_PIECES[i]
        cut = pl.ds(start, width)
        await_bytes(q_r.at[:, cut], b3_sem.at[i])
        total = q_r[0:TOK, cut].astype(F32)
        for k in range(1, 4):
            total += q_r[k * TOK : (k + 1) * TOK, cut].astype(F32)
        out[:, cut] = total.astype(BF16)

    count = len(OUT_PIECES)
    gather(0)
    for i in range(count):
        for copy in weight_copies(i):
            copy.start()
    gather(1)
    choose_tokens()
    for s in range(count + 2):
        if s < count:
            spread(s)
            if s + 2 < count:
                gather(s + 2)
        if s == 0:
            choose_slots()
        if 0 <= s - 1 < count:
            forward(s - 1)
        if 0 <= s - 2 < count:
            multiply(s - 2)
    activate()
    count = len(BACK_PIECES)
    for s in range(count + 3):
        if s < count:
            back_rows(s)
        if 0 <= s - 1 < count:
            back_slots(s - 1)
        if 0 <= s - 2 < count:
            back_tokens(s - 2)
        if 0 <= s - 3 < count:
            finish(s - 3)

    for p in (0, 1):
        await_bytes(metas[p].at[0:48, :], send_sem.at[p])
        await_bytes(gathered[p].at[0:48, :], send_sem.at[4 + p])
        await_bytes(spread_s[p].at[0:112, :], send_sem.at[6 + p])
    await_bytes(m_s.at[0:112, :], send_sem.at[2])
    await_bytes(mx_s.at[0:96, :], send_sem.at[3])
    await_bytes(x_s.at[0:96, :], send_sem.at[8])
    await_bytes(y_s.at[0:96, :], send_sem.at[9])
    await_bytes(u_s.at[0:112, :], send_sem.at[10])
    await_bytes(q_s.at[0:48, :], send_sem.at[11])


def local(layer_input, grad_output, expert_ids, route_weights, w_gate, w_up, w_down):
    vmem = pl.BlockSpec(memory_space=pltpu.VMEM)
    anywhere = pl.BlockSpec(memory_space=pl.ANY)
    dma = pltpu.SemaphoreType.DMA
    n_out, n_back = len(OUT_PIECES), len(BACK_PIECES)

    def buf(*shape):
        return pltpu.VMEM(shape, BF16)

    scratch = [
        buf(D, HW),
        buf(D, HW),
        buf(HW, D),
        buf(TOK, 128),
        buf(64, 128),
        buf(64, 128),
        buf(128, 128),
        buf(128, 128),
        buf(128, 128),
        buf(128, 128),
        buf(64, D),
        buf(64, D),
        buf(128, D),
        buf(128, D),
        buf(128, D),
        buf(128, D),
        buf(128, 2 * D),
        buf(128, 2 * D),
        buf(128, 64),
        buf(128, 64),
        buf(64, 128),
        buf(64, 128),
        buf(128, 128),
        buf(128, 128),
        buf(128, 128),
        buf(128, 128),
        pltpu.VMEM((128, HW), F32),
        pltpu.VMEM((128, HW), F32),
        pltpu.VMEM((128, HW), F32),
        buf(128, HW),
        buf(128, HW),
        buf(128, D),
        buf(128, D),
        buf(128, D),
        buf(128, D),
        buf(64, D),
        buf(64, D),
        dma((3, n_out)),
        dma((4,)),
        dma((2, n_out)),
        dma((2, n_out)),
        dma((n_out,)),
        dma((n_back,)),
        dma((n_back,)),
        dma((n_back,)),
        dma((12,)),
    ]
    return pl.pallas_call(
        kernel,
        out_shape=jax.ShapeDtypeStruct((TOK, D), BF16),
        in_specs=[anywhere, anywhere, vmem, vmem, anywhere, anywhere, anywhere],
        out_specs=vmem,
        scratch_shapes=scratch,
        compiler_params=pltpu.CompilerParams(
            collective_id=0, has_side_effects=True, vmem_limit_bytes=60 * 2**20
        ),
    )(layer_input, grad_output, expert_ids, route_weights, w_gate, w_up, w_down)


def solution(mesh):
    both = ("node", "local")
    return jax.shard_map(
        local,
        mesh=mesh,
        in_specs=(
            P(both, None),
            P(both, None),
            P(both, None),
            P(both, None),
            P(both, None, None),
            P(both, None, None),
            P(both, None, None),
        ),
        out_specs=P(both, None),
        check_vma=False,
    )
```

```python
import jax
import jax.numpy as jnp
from jax import lax
from jax.experimental import pallas as pl
from jax.experimental.pallas import tpu as pltpu
from jax.sharding import PartitionSpec as P

MESH = pl.DeviceIdType.MESH
BF16 = jnp.bfloat16
F32 = jnp.float32

D = 3584
HW = 1024
TOK = 16
OUT_CUTS = (512, 768, 768, 768, 512, 256)
BACK_CUTS = (512,) * 7
HB = 512
NB = 256


def pieces(cuts):
    starts = [sum(cuts[:i]) for i in range(len(cuts))]
    return tuple(zip(starts, cuts))


OUT_PIECES = pieces(OUT_CUTS)
BACK_PIECES = pieces(BACK_CUTS)


OUT_LAGS = (-3, 0, 2, 4)
BACK_LAGS = (0, 4, 7, 10)


def run_in_order(count, stages, lags, before):
    order = sorted((i + lag, k, i) for k, lag in enumerate(lags) for i in range(count))
    for _, k, i in order:
        if (i, k) in before:
            before[(i, k)]()
        stages[k](i)


def iota(shape, dim):
    return lax.broadcasted_iota(jnp.int32, shape, dim)


def dot(a, b):
    return jnp.dot(a, b, preferred_element_type=F32)


def dot_t(a, b):
    return lax.dot_general(a, b, (((1,), (1,)), ((), ())), preferred_element_type=F32)


def as01(mask):
    return jnp.where(mask, 1.0, 0.0).astype(BF16)


def rows(start, size):
    return pl.ds(pl.multiple_of(start, size), size)


def kernel(
    x_in,
    g_in,
    ids,
    route,
    wg_hbm,
    wu_hbm,
    wd_hbm,
    q_r,
    wg,
    wu,
    wd,
    w_tok,
    m1,
    m2,
    m_s,
    m_r,
    mx_s,
    mx_r,
    a1,
    a2,
    s1,
    s2,
    r1,
    r2,
    x_s,
    x_r,
    sel1,
    sel2,
    sel1t,
    sel2t,
    pick1,
    pick2,
    pick1t,
    pick2t,
    want1,
    want2,
    want_x,
    pre_gate,
    pre_up,
    hidden,
    d_gate,
    d_up,
    y_s,
    y_r,
    u_s,
    u_r,
    q_s,
    w_sem,
    meta_sem,
    h1_sem,
    h2_sem,
    x_sem,
    b1_sem,
    b2_sem,
    b3_sem,
    send_sem,
):
    node = lax.axis_index("node")
    xi = lax.axis_index("local")
    yi, zi, ci = node // 8, lax.rem(node // 2, 4), lax.rem(node, 2)

    def turn(v, k, size):
        return lax.rem(v + k, size)

    def device(y, z, c, x):
        return (y * 8 + z * 2 + c, x)

    far_first = (2, 1, 3)
    y_line = [(turn(yi, k, 4), device(turn(yi, k, 4), zi, ci, xi)) for k in far_first]
    z_line = [(turn(zi, k, 4), device(yi, turn(zi, k, 4), ci, xi)) for k in far_first]
    x_line = [(turn(xi, k, 4), device(yi, zi, ci, turn(xi, k, 4))) for k in far_first]
    steps = [(k, c) for k in far_first for c in (0, 1)] + [(0, 1)]
    zc_plane = [
        (turn(zi, k, 4) * 2 + turn(ci, c, 2), device(yi, turn(zi, k, 4), turn(ci, c, 2), xi))
        for k, c in steps
    ]
    yc_plane = [
        (turn(yi, k, 4) * 2 + turn(ci, c, 2), device(turn(yi, k, 4), zi, turn(ci, c, 2), xi))
        for k, c in steps
    ]
    lines = (y_line, z_line)
    planes = (zc_plane, yc_plane)
    line_at = (yi, zi)
    plane_at = (zi * 2 + ci, yi * 2 + ci)

    def local_copy(src, dst, sem):
        pltpu.make_async_copy(src, dst, sem).start()

    def remote_copy(src, dst, sem, send, target):
        pltpu.make_async_remote_copy(
            src_ref=src,
            dst_ref=dst,
            send_sem=send_sem.at[send],
            recv_sem=sem,
            device_id=target,
            device_id_type=MESH,
        ).start()

    def await_bytes(ref, sem):
        pltpu.make_async_copy(ref, ref, sem).wait()

    def weight_copies(i):
        start, width = OUT_PIECES[i]
        cut = pl.ds(start, width)
        return (
            pltpu.make_async_copy(wg_hbm.at[0, cut, :], wg.at[cut, :], w_sem.at[0, i]),
            pltpu.make_async_copy(wu_hbm.at[0, cut, :], wu.at[cut, :], w_sem.at[1, i]),
            pltpu.make_async_copy(wd_hbm.at[0, :, cut], wd.at[:, cut], w_sem.at[2, i]),
        )

    barrier = pltpu.get_barrier_semaphore()
    partners = [d for _, d in zc_plane] + [d for _, d in yc_plane[:-1]] + [d for _, d in x_line]
    for target in partners:
        pl.semaphore_signal(barrier, inc=1, device_id=target, device_id_type=MESH)

    for i in range(len(OUT_PIECES)):
        for copy in weight_copies(i):
            copy.start()

    down = iota((128, TOK), 0)
    table_t = jnp.zeros((128, TOK), F32)
    id_block, route_block = ids[...], route[...].astype(F32)
    for k in range(8):
        table_t += jnp.where(id_block[k : k + 1, :] == down, route_block[k : k + 1, :], 0.0)
    small0, small1 = iota((TOK, TOK), 0), iota((TOK, TOK), 1)
    table = dot_t(as01(small0 == small1), table_t.astype(BF16))
    row, col = iota((128, 128), 0), iota((128, 128), 1)
    in_group = dot(as01(table > 0), as01((row >> 2) == (col >> 2))) > 0.5
    rank = dot(as01(small1 < small0), as01(in_group))
    w_tok[:, 0:128] = table.astype(BF16)
    w_tok[:, 128:256] = jnp.where(in_group, rank + 1.0, 0.0).astype(BF16)
    first = (col & 3) == 0
    group = col >> 2
    place = row >> 4
    want1[...] = as01(first & ((group >> 3) == yi) & ((group & 7) == place))
    want2[...] = as01(
        first & (((group >> 1) & 3) == zi) & (((group >> 3) * 2 + (group & 1)) == place)
    )
    want_x[...] = as01(col == node * 4 + (row >> 5))

    pl.semaphore_wait(barrier, len(partners))

    metas = (m1, m2)
    gathered = (a1, a2)
    sources = (x_in, g_in)
    spread_s, spread_r = (s1, s2), (r1, r2)
    sel, sel_t = (sel1, sel2), (sel1t, sel2t)
    pick, pick_t = (pick1, pick2), (pick1t, pick2t)
    wants = (want1, want2)

    for p in (0, 1):
        mine = metas[p].at[rows(line_at[p] * TOK, TOK), :]
        for _, target in lines[p]:
            remote_copy(w_tok, mine, meta_sem.at[p], p, target)
        local_copy(w_tok, mine, meta_sem.at[p])

    def gather(i):
        start, width = OUT_PIECES[i]
        cut = pl.ds(start, width)
        for p in (0, 1):
            mine = gathered[p].at[rows(line_at[p] * TOK, TOK), cut]
            for _, target in lines[p]:
                remote_copy(sources[p].at[:, cut], mine, h1_sem.at[p, i], 4 + p, target)
            local_copy(sources[p].at[:, cut], mine, h1_sem.at[p, i])

    def spread(i):
        start, width = OUT_PIECES[i]
        cut = pl.ds(start, width)
        for p in (0, 1):
            await_bytes(gathered[p].at[:, cut], h1_sem.at[p, i])
            spread_s[p][:, cut] = dot(sel[p][...], gathered[p][:, cut]).astype(BF16)
            mine = rows(plane_at[p] * TOK, TOK)
            for at, target in planes[p]:
                remote_copy(
                    spread_s[p].at[rows(at * TOK, TOK), cut],
                    spread_r[p].at[mine, cut],
                    h2_sem.at[p, i],
                    6 + p,
                    target,
                )
            local_copy(spread_s[p].at[mine, cut], spread_r[p].at[mine, cut], h2_sem.at[p, i])

    def forward(i):
        start, width = OUT_PIECES[i]
        cut = pl.ds(start, width)
        for p in (0, 1):
            await_bytes(spread_r[p].at[:, cut], h2_sem.at[p, i])
            x_s[:, pl.ds(2 * start + p * width, width)] = dot(
                pick[p][...], spread_r[p][:, cut]
            ).astype(BF16)
        both = pl.ds(2 * start, 2 * width)
        mine = rows(xi * 32, 32)
        for at, target in x_line:
            remote_copy(x_s.at[rows(at * 32, 32), both], x_r.at[mine, both], x_sem.at[i], 8, target)
        local_copy(x_s.at[mine, both], x_r.at[mine, both], x_sem.at[i])

    def multiply(i):
        start, width = OUT_PIECES[i]
        cut = pl.ds(start, width)
        both = pl.ds(2 * start, 2 * width)
        for copy in weight_copies(i):
            copy.wait()
        await_bytes(x_r.at[:, both], x_sem.at[i])
        x_part = x_r[:, pl.ds(2 * start, width)]
        g_part = x_r[:, pl.ds(2 * start + width, width)]

        @pl.loop(0, HW // HB)
        def _(n):
            block = rows(n * HB, HB)
            gate = dot(x_part, wg[cut, block])
            up = dot(x_part, wu[cut, block])
            hid = dot_t(g_part, wd[block, cut])
            if i == 0:
                pre_gate[:, block] = gate
                pre_up[:, block] = up
                hidden[:, block] = hid
            else:
                pre_gate[:, block] += gate
                pre_up[:, block] += up
                hidden[:, block] += hid

    def choose_tokens():
        r0, c0 = iota((128, 64), 0), iota((128, 64), 1)
        fits = ((r0 >> 2) & 3) == (c0 >> 4)
        slot = ((r0 & 3) + 1).astype(F32)
        for p in (0, 1):
            await_bytes(metas[p], meta_sem.at[p])
        for p in (0, 1):
            found = dot_t(wants[p][...], metas[p][:, 128:256])
            sel[p][...] = as01(fits & (found == slot))
        m_s[...] = dot(sel1[...], m1[:, 0:128]).astype(BF16)
        mine = rows(plane_at[0] * TOK, TOK)
        for at, target in planes[0]:
            remote_copy(m_s.at[rows(at * TOK, TOK), :], m_r.at[mine, :], meta_sem.at[2], 2, target)
        local_copy(m_s.at[mine, :], m_r.at[mine, :], meta_sem.at[2])

    def choose_slots():
        row, col = iota((128, 128), 0), iota((128, 128), 1)
        await_bytes(m_r, meta_sem.at[2])
        hits = as01(m_r[...].astype(F32) > 0)
        hit = dot_t(want_x[...], hits) > 0.5
        rank = dot(as01(hit), as01(row < col)).astype(jnp.int32)
        p1 = as01(hit & (rank == (row & 31)))
        pick1[...] = p1
        pick2[...] = dot(p1, as01(swapped(row) == col)).astype(BF16)

    def swapped(slot):
        return ((slot >> 2) & 3) * 32 + (slot & 16) + (slot >> 5) * 4 + (slot & 3)

    def choose_late():
        mx_s[...] = dot(pick1[...], m_r[...]).astype(BF16)
        mine = rows(xi * 32, 32)
        for at, target in x_line:
            remote_copy(mx_s.at[rows(at * 32, 32), :], mx_r.at[mine, :], meta_sem.at[3], 3, target)
        local_copy(mx_s.at[mine, :], mx_r.at[mine, :], meta_sem.at[3])
        row, col = iota((128, 128), 0), iota((128, 128), 1)
        same = as01(row == col)
        p1t = dot_t(same, pick1[...]).astype(BF16)
        pick1t[...] = p1t
        pick2t[...] = dot(as01(swapped(row) == col), p1t).astype(BF16)
        for p in (0, 1):
            sel_t[p][...] = dot_t(same[0:64, 0:64], sel[p][...]).astype(BF16)

    def activate():
        await_bytes(mx_r, meta_sem.at[3])
        scale = jnp.sum(
            jnp.where(iota((128, 128), 1) == node * 4 + xi, mx_r[...].astype(F32), 0.0),
            axis=1,
            keepdims=True,
        )

        @pl.loop(0, HW // NB)
        def _(n):
            block = rows(n * NB, NB)
            gate, up = pre_gate[:, block], pre_up[:, block]
            grad = scale * hidden[:, block]
            s = jax.nn.sigmoid(gate)
            d_gate[:, block] = (grad * up * s * (1.0 + gate * (1.0 - s))).astype(BF16)
            d_up[:, block] = (grad * gate * s).astype(BF16)

    def back_rows(i):
        start, width = BACK_PIECES[i]
        cut = pl.ds(start, width)

        @pl.loop(0, width // NB)
        def _(n):
            block = rows(start + n * NB, NB)
            total = dot_t(d_gate[...], wg[block, :]) + dot_t(d_up[...], wu[block, :])
            y_s[:, block] = total.astype(BF16)

        mine = rows(xi * 32, 32)
        for at, target in x_line:
            remote_copy(y_s.at[rows(at * 32, 32), cut], y_r.at[mine, cut], b1_sem.at[i], 9, target)
        local_copy(y_s.at[mine, cut], y_r.at[mine, cut], b1_sem.at[i])

    def back_slots(i):
        start, width = BACK_PIECES[i]
        cut = pl.ds(start, width)
        p = i % 2
        await_bytes(y_r.at[:, cut], b1_sem.at[i])
        u_s[:, cut] = dot(pick_t[p][...], y_r[:, cut]).astype(BF16)
        mine = rows(plane_at[p] * TOK, TOK)
        for at, target in planes[p]:
            remote_copy(
                u_s.at[rows(at * TOK, TOK), cut], u_r.at[mine, cut], b2_sem.at[i], 10, target
            )
        local_copy(u_s.at[mine, cut], u_r.at[mine, cut], b2_sem.at[i])

    def back_tokens(i):
        start, width = BACK_PIECES[i]
        cut = pl.ds(start, width)
        p = i % 2
        await_bytes(u_r.at[:, cut], b2_sem.at[i])
        q_s[:, cut] = dot(sel_t[p][...], u_r[:, cut]).astype(BF16)
        mine = rows(line_at[p] * TOK, TOK)
        for at, target in lines[p]:
            remote_copy(
                q_s.at[rows(at * TOK, TOK), cut], q_r.at[mine, cut], b3_sem.at[i], 11, target
            )
        local_copy(q_s.at[mine, cut], q_r.at[mine, cut], b3_sem.at[i])

    def finish(i):
        start, width = BACK_PIECES[i]
        await_bytes(q_r.at[:, pl.ds(start, width)], b3_sem.at[i])

    out_extra = {
        (0, 1): choose_tokens,
        (0, 2): choose_slots,
        (0, 3): choose_late,
    }
    run_in_order(len(OUT_PIECES), (gather, spread, forward, multiply), OUT_LAGS, out_extra)
    activate()
    run_in_order(len(BACK_PIECES), (back_rows, back_slots, back_tokens, finish), BACK_LAGS, {})

    for p in (0, 1):
        await_bytes(metas[p].at[0:48, :], send_sem.at[p])
        await_bytes(gathered[p].at[0:48, :], send_sem.at[4 + p])
        await_bytes(spread_s[p].at[0:112, :], send_sem.at[6 + p])
    await_bytes(m_s.at[0:112, :], send_sem.at[2])
    await_bytes(mx_s.at[0:96, :], send_sem.at[3])
    await_bytes(x_s.at[0:96, :], send_sem.at[8])
    await_bytes(y_s.at[0:96, :], send_sem.at[9])
    await_bytes(u_s.at[0:112, :], send_sem.at[10])
    await_bytes(q_s.at[0:48, :], send_sem.at[11])


def local(layer_input, grad_output, expert_ids, route_weights, w_gate, w_up, w_down):
    vmem = pl.BlockSpec(memory_space=pltpu.VMEM)
    anywhere = pl.BlockSpec(memory_space=pl.ANY)
    dma = pltpu.SemaphoreType.DMA
    n_out, n_back = len(OUT_PIECES), len(BACK_PIECES)

    def buf(*shape):
        return pltpu.VMEM(shape, BF16)

    scratch = [
        buf(D, HW),
        buf(D, HW),
        buf(HW, D),
        buf(TOK, 256),
        buf(64, 256),
        buf(64, 256),
        buf(128, 128),
        buf(128, 128),
        buf(128, 128),
        buf(128, 128),
        buf(64, D),
        buf(64, D),
        buf(128, D),
        buf(128, D),
        buf(128, D),
        buf(128, D),
        buf(128, 2 * D),
        buf(128, 2 * D),
        buf(128, 64),
        buf(128, 64),
        buf(64, 128),
        buf(64, 128),
        buf(128, 128),
        buf(128, 128),
        buf(128, 128),
        buf(128, 128),
        buf(128, 128),
        buf(128, 128),
        buf(128, 128),
        pltpu.VMEM((128, HW), F32),
        pltpu.VMEM((128, HW), F32),
        pltpu.VMEM((128, HW), F32),
        buf(128, HW),
        buf(128, HW),
        buf(128, D),
        buf(128, D),
        buf(128, D),
        buf(128, D),
        buf(64, D),
        dma((3, n_out)),
        dma((4,)),
        dma((2, n_out)),
        dma((2, n_out)),
        dma((n_out,)),
        dma((n_back,)),
        dma((n_back,)),
        dma((n_back,)),
        dma((12,)),
    ]
    parts = pl.pallas_call(
        kernel,
        out_shape=jax.ShapeDtypeStruct((4 * TOK, D), BF16),
        in_specs=[anywhere, anywhere, vmem, vmem, anywhere, anywhere, anywhere],
        out_specs=anywhere,
        scratch_shapes=scratch,
        compiler_params=pltpu.CompilerParams(
            collective_id=0, has_side_effects=True, vmem_limit_bytes=60 * 2**20
        ),
    )(layer_input, grad_output, expert_ids.T, route_weights.T, w_gate, w_up, w_down)
    return jnp.sum(parts.reshape(4, TOK, D).astype(F32), axis=0).astype(BF16)


def solution(mesh):
    both = ("node", "local")
    return jax.shard_map(
        local,
        mesh=mesh,
        in_specs=(
            P(both, None),
            P(both, None),
            P(both, None),
            P(both, None),
            P(both, None, None),
            P(both, None, None),
            P(both, None, None),
        ),
        out_specs=P(both, None),
        check_vma=False,
    )
```

```python
import jax
import jax.numpy as jnp
from jax import lax
from jax.experimental import pallas as pl
from jax.experimental.pallas import tpu as pltpu
from jax.sharding import PartitionSpec as P

MESH = pl.DeviceIdType.MESH
BF16 = jnp.bfloat16
F32 = jnp.float32

D = 3584
HW = 1024
TOK = 16
OUT_CUTS = (512, 768, 768, 768, 512, 256)
BACK_CUTS = (512,) * 7
HB = 1024
RB = 512
NB = 256


def pieces(cuts):
    starts = [sum(cuts[:i]) for i in range(len(cuts))]
    return tuple(zip(starts, cuts))


OUT_PIECES = pieces(OUT_CUTS)
BACK_PIECES = pieces(BACK_CUTS)


OUT_LAGS = (-3, 0, 1, 3)
BACK_LAGS = (0, 4, 7, 10)


def run_in_order(count, stages, lags, before):
    order = sorted((i + lag, k, i) for k, lag in enumerate(lags) for i in range(count))
    for _, k, i in order:
        if (i, k) in before:
            before[(i, k)]()
        stages[k](i)


def iota(shape, dim):
    return lax.broadcasted_iota(jnp.int32, shape, dim)


def dot(a, b):
    return jnp.dot(a, b, preferred_element_type=F32)


def dot_t(a, b):
    return lax.dot_general(a, b, (((1,), (1,)), ((), ())), preferred_element_type=F32)


def as01(mask):
    return jnp.where(mask, 1.0, 0.0).astype(BF16)


def rows(start, size):
    return pl.ds(pl.multiple_of(start, size), size)


def kernel(
    x_in,
    g_in,
    ids,
    route,
    wg_hbm,
    wu_hbm,
    wd_hbm,
    q_r,
    wg,
    wu,
    wd,
    w_tok,
    m1,
    m2,
    m_s,
    m_r,
    mx_s,
    mx_r,
    a1,
    a2,
    s1,
    s2,
    r1,
    r2,
    x_s,
    x_r,
    sel1,
    sel2,
    sel1t,
    sel2t,
    pick1,
    pick2,
    pick1t,
    pick2t,
    want1,
    want2,
    want_x,
    pre_gate,
    pre_up,
    hidden,
    d_gate,
    d_up,
    y_s,
    y_r,
    u_s,
    u_r,
    q_s,
    w_sem,
    meta_sem,
    h1_sem,
    h2_sem,
    x_sem,
    b1_sem,
    b2_sem,
    b3_sem,
    send_sem,
):
    node = lax.axis_index("node")
    xi = lax.axis_index("local")
    yi, zi, ci = node // 8, lax.rem(node // 2, 4), lax.rem(node, 2)

    def turn(v, k, size):
        return lax.rem(v + k, size)

    def device(y, z, c, x):
        return (y * 8 + z * 2 + c, x)

    far_first = (2, 1, 3)
    y_line = [(turn(yi, k, 4), device(turn(yi, k, 4), zi, ci, xi)) for k in far_first]
    z_line = [(turn(zi, k, 4), device(yi, turn(zi, k, 4), ci, xi)) for k in far_first]
    x_line = [(turn(xi, k, 4), device(yi, zi, ci, turn(xi, k, 4))) for k in far_first]
    steps = [(k, c) for k in far_first for c in (0, 1)] + [(0, 1)]
    zc_plane = [
        (turn(zi, k, 4) * 2 + turn(ci, c, 2), device(yi, turn(zi, k, 4), turn(ci, c, 2), xi))
        for k, c in steps
    ]
    yc_plane = [
        (turn(yi, k, 4) * 2 + turn(ci, c, 2), device(turn(yi, k, 4), zi, turn(ci, c, 2), xi))
        for k, c in steps
    ]
    lines = (y_line, z_line)
    planes = (zc_plane, yc_plane)
    line_at = (yi, zi)
    plane_at = (zi * 2 + ci, yi * 2 + ci)

    def local_copy(src, dst, sem):
        pltpu.make_async_copy(src, dst, sem).start()

    def remote_copy(src, dst, sem, send, target):
        pltpu.make_async_remote_copy(
            src_ref=src,
            dst_ref=dst,
            send_sem=send_sem.at[send],
            recv_sem=sem,
            device_id=target,
            device_id_type=MESH,
        ).start()

    def await_bytes(ref, sem):
        pltpu.make_async_copy(ref, ref, sem).wait()

    def weight_copies(i):
        start, width = OUT_PIECES[i]
        cut = pl.ds(start, width)
        return (
            pltpu.make_async_copy(wg_hbm.at[0, cut, :], wg.at[cut, :], w_sem.at[0, i]),
            pltpu.make_async_copy(wu_hbm.at[0, cut, :], wu.at[cut, :], w_sem.at[1, i]),
            pltpu.make_async_copy(wd_hbm.at[0, :, cut], wd.at[:, cut], w_sem.at[2, i]),
        )

    barrier = pltpu.get_barrier_semaphore()
    partners = [d for _, d in zc_plane] + [d for _, d in yc_plane[:-1]] + [d for _, d in x_line]
    for target in partners:
        pl.semaphore_signal(barrier, inc=1, device_id=target, device_id_type=MESH)

    for i in range(len(OUT_PIECES)):
        for copy in weight_copies(i):
            copy.start()

    down = iota((128, TOK), 0)
    table_t = jnp.zeros((128, TOK), F32)
    id_block, route_block = ids[...], route[...].astype(F32)
    for k in range(8):
        table_t += jnp.where(id_block[k : k + 1, :] == down, route_block[k : k + 1, :], 0.0)
    small0, small1 = iota((TOK, TOK), 0), iota((TOK, TOK), 1)
    table = dot_t(as01(small0 == small1), table_t.astype(BF16))
    row, col = iota((128, 128), 0), iota((128, 128), 1)
    in_group = dot(as01(table > 0), as01((row >> 2) == (col >> 2))) > 0.5
    rank = dot(as01(small1 < small0), as01(in_group))
    w_tok[:, 0:128] = table.astype(BF16)
    w_tok[:, 128:256] = jnp.where(in_group, rank + 1.0, 0.0).astype(BF16)
    first = (col & 3) == 0
    group = col >> 2
    place = row >> 4
    want1[...] = as01(first & ((group >> 3) == yi) & ((group & 7) == place))
    want2[...] = as01(
        first & (((group >> 1) & 3) == zi) & (((group >> 3) * 2 + (group & 1)) == place)
    )
    want_x[...] = as01(col == node * 4 + (row >> 5))

    pl.semaphore_wait(barrier, len(partners))

    metas = (m1, m2)
    gathered = (a1, a2)
    sources = (x_in, g_in)
    spread_s, spread_r = (s1, s2), (r1, r2)
    sel, sel_t = (sel1, sel2), (sel1t, sel2t)
    pick, pick_t = (pick1, pick2), (pick1t, pick2t)
    wants = (want1, want2)

    for p in (0, 1):
        mine = metas[p].at[rows(line_at[p] * TOK, TOK), :]
        for _, target in lines[p]:
            remote_copy(w_tok, mine, meta_sem.at[p], p, target)
        local_copy(w_tok, mine, meta_sem.at[p])

    def gather(i):
        start, width = OUT_PIECES[i]
        cut = pl.ds(start, width)
        for p in (0, 1):
            mine = gathered[p].at[rows(line_at[p] * TOK, TOK), cut]
            for _, target in lines[p]:
                remote_copy(sources[p].at[:, cut], mine, h1_sem.at[p, i], 4 + p, target)
            local_copy(sources[p].at[:, cut], mine, h1_sem.at[p, i])

    def spread(i):
        start, width = OUT_PIECES[i]
        cut = pl.ds(start, width)
        for p in (0, 1):
            await_bytes(gathered[p].at[:, cut], h1_sem.at[p, i])
            spread_s[p][:, cut] = dot(sel[p][...], gathered[p][:, cut]).astype(BF16)
            mine = rows(plane_at[p] * TOK, TOK)
            for at, target in planes[p]:
                remote_copy(
                    spread_s[p].at[rows(at * TOK, TOK), cut],
                    spread_r[p].at[mine, cut],
                    h2_sem.at[p, i],
                    6 + p,
                    target,
                )
            local_copy(spread_s[p].at[mine, cut], spread_r[p].at[mine, cut], h2_sem.at[p, i])

    def forward(i):
        start, width = OUT_PIECES[i]
        cut = pl.ds(start, width)
        for p in (0, 1):
            await_bytes(spread_r[p].at[:, cut], h2_sem.at[p, i])
            x_s[:, pl.ds(2 * start + p * width, width)] = dot(
                pick[p][...], spread_r[p][:, cut]
            ).astype(BF16)
        both = pl.ds(2 * start, 2 * width)
        mine = rows(xi * 32, 32)
        for at, target in x_line:
            remote_copy(x_s.at[rows(at * 32, 32), both], x_r.at[mine, both], x_sem.at[i], 8, target)
        local_copy(x_s.at[mine, both], x_r.at[mine, both], x_sem.at[i])

    def multiply(i):
        start, width = OUT_PIECES[i]
        cut = pl.ds(start, width)
        both = pl.ds(2 * start, 2 * width)
        for copy in weight_copies(i):
            copy.wait()
        await_bytes(x_r.at[:, both], x_sem.at[i])
        x_part = x_r[:, pl.ds(2 * start, width)]
        g_part = x_r[:, pl.ds(2 * start + width, width)]

        @pl.loop(0, HW // HB)
        def _(n):
            block = rows(n * HB, HB)
            gate = dot(x_part, wg[cut, block])
            up = dot(x_part, wu[cut, block])
            hid = dot_t(g_part, wd[block, cut])
            if i == 0:
                pre_gate[:, block] = gate
                pre_up[:, block] = up
                hidden[:, block] = hid
            else:
                pre_gate[:, block] += gate
                pre_up[:, block] += up
                hidden[:, block] += hid

    def choose_tokens():
        r0, c0 = iota((128, 64), 0), iota((128, 64), 1)
        fits = ((r0 >> 2) & 3) == (c0 >> 4)
        slot = ((r0 & 3) + 1).astype(F32)
        for p in (0, 1):
            await_bytes(metas[p], meta_sem.at[p])
        for p in (0, 1):
            found = dot_t(wants[p][...], metas[p][:, 128:256])
            sel[p][...] = as01(fits & (found == slot))
        m_s[...] = dot(sel1[...], m1[:, 0:128]).astype(BF16)
        mine = rows(plane_at[0] * TOK, TOK)
        for at, target in planes[0]:
            remote_copy(m_s.at[rows(at * TOK, TOK), :], m_r.at[mine, :], meta_sem.at[2], 2, target)
        local_copy(m_s.at[mine, :], m_r.at[mine, :], meta_sem.at[2])

    def choose_slots():
        row, col = iota((128, 128), 0), iota((128, 128), 1)
        await_bytes(m_r, meta_sem.at[2])
        hits = as01(m_r[...].astype(F32) > 0)
        hit = dot_t(want_x[...], hits) > 0.5
        rank = dot(as01(hit), as01(row < col)).astype(jnp.int32)
        p1 = as01(hit & (rank == (row & 31)))
        pick1[...] = p1
        pick2[...] = dot(p1, as01(swapped(row) == col)).astype(BF16)

    def swapped(slot):
        return ((slot >> 2) & 3) * 32 + (slot & 16) + (slot >> 5) * 4 + (slot & 3)

    def choose_late():
        mx_s[...] = dot(pick1[...], m_r[...]).astype(BF16)
        mine = rows(xi * 32, 32)
        for at, target in x_line:
            remote_copy(mx_s.at[rows(at * 32, 32), :], mx_r.at[mine, :], meta_sem.at[3], 3, target)
        local_copy(mx_s.at[mine, :], mx_r.at[mine, :], meta_sem.at[3])
        row, col = iota((128, 128), 0), iota((128, 128), 1)
        same = as01(row == col)
        p1t = dot_t(same, pick1[...]).astype(BF16)
        pick1t[...] = p1t
        pick2t[...] = dot(as01(swapped(row) == col), p1t).astype(BF16)
        for p in (0, 1):
            sel_t[p][...] = dot_t(same[0:64, 0:64], sel[p][...]).astype(BF16)

    def activate():
        await_bytes(mx_r, meta_sem.at[3])
        scale = jnp.sum(
            jnp.where(iota((128, 128), 1) == node * 4 + xi, mx_r[...].astype(F32), 0.0),
            axis=1,
            keepdims=True,
        )

        @pl.loop(0, HW // NB)
        def _(n):
            block = rows(n * NB, NB)
            gate, up = pre_gate[:, block], pre_up[:, block]
            grad = scale * hidden[:, block]
            s = jax.nn.sigmoid(gate)
            d_gate[:, block] = (grad * up * s * (1.0 + gate * (1.0 - s))).astype(BF16)
            d_up[:, block] = (grad * gate * s).astype(BF16)

    def back_rows(i):
        start, width = BACK_PIECES[i]
        cut = pl.ds(start, width)

        @pl.loop(0, width // RB)
        def _(n):
            block = rows(start + n * RB, RB)
            total = dot_t(d_gate[...], wg[block, :]) + dot_t(d_up[...], wu[block, :])
            y_s[:, block] = total.astype(BF16)

        mine = rows(xi * 32, 32)
        for at, target in x_line:
            remote_copy(y_s.at[rows(at * 32, 32), cut], y_r.at[mine, cut], b1_sem.at[i], 9, target)
        local_copy(y_s.at[mine, cut], y_r.at[mine, cut], b1_sem.at[i])

    def back_slots(i):
        start, width = BACK_PIECES[i]
        cut = pl.ds(start, width)
        p = i % 2
        await_bytes(y_r.at[:, cut], b1_sem.at[i])
        u_s[:, cut] = dot(pick_t[p][...], y_r[:, cut]).astype(BF16)
        mine = rows(plane_at[p] * TOK, TOK)
        for at, target in planes[p]:
            remote_copy(
                u_s.at[rows(at * TOK, TOK), cut], u_r.at[mine, cut], b2_sem.at[i], 10, target
            )
        local_copy(u_s.at[mine, cut], u_r.at[mine, cut], b2_sem.at[i])

    def back_tokens(i):
        start, width = BACK_PIECES[i]
        cut = pl.ds(start, width)
        p = i % 2
        await_bytes(u_r.at[:, cut], b2_sem.at[i])
        q_s[:, cut] = dot(sel_t[p][...], u_r[:, cut]).astype(BF16)
        mine = rows(line_at[p] * TOK, TOK)
        for at, target in lines[p]:
            remote_copy(
                q_s.at[rows(at * TOK, TOK), cut], q_r.at[mine, cut], b3_sem.at[i], 11, target
            )
        local_copy(q_s.at[mine, cut], q_r.at[mine, cut], b3_sem.at[i])

    def finish(i):
        start, width = BACK_PIECES[i]
        await_bytes(q_r.at[:, pl.ds(start, width)], b3_sem.at[i])

    out_extra = {
        (0, 1): choose_tokens,
        (0, 2): choose_slots,
        (0, 3): choose_late,
    }
    run_in_order(len(OUT_PIECES), (gather, spread, forward, multiply), OUT_LAGS, out_extra)
    activate()
    run_in_order(len(BACK_PIECES), (back_rows, back_slots, back_tokens, finish), BACK_LAGS, {})

    for p in (0, 1):
        await_bytes(metas[p].at[0:48, :], send_sem.at[p])
        await_bytes(gathered[p].at[0:48, :], send_sem.at[4 + p])
        await_bytes(spread_s[p].at[0:112, :], send_sem.at[6 + p])
    await_bytes(m_s.at[0:112, :], send_sem.at[2])
    await_bytes(mx_s.at[0:96, :], send_sem.at[3])
    await_bytes(x_s.at[0:96, :], send_sem.at[8])
    await_bytes(y_s.at[0:96, :], send_sem.at[9])
    await_bytes(u_s.at[0:112, :], send_sem.at[10])
    await_bytes(q_s.at[0:48, :], send_sem.at[11])


def local(layer_input, grad_output, expert_ids, route_weights, w_gate, w_up, w_down):
    vmem = pl.BlockSpec(memory_space=pltpu.VMEM)
    anywhere = pl.BlockSpec(memory_space=pl.ANY)
    dma = pltpu.SemaphoreType.DMA
    n_out, n_back = len(OUT_PIECES), len(BACK_PIECES)

    def buf(*shape):
        return pltpu.VMEM(shape, BF16)

    scratch = [
        buf(D, HW),
        buf(D, HW),
        buf(HW, D),
        buf(TOK, 256),
        buf(64, 256),
        buf(64, 256),
        buf(128, 128),
        buf(128, 128),
        buf(128, 128),
        buf(128, 128),
        buf(64, D),
        buf(64, D),
        buf(128, D),
        buf(128, D),
        buf(128, D),
        buf(128, D),
        buf(128, 2 * D),
        buf(128, 2 * D),
        buf(128, 64),
        buf(128, 64),
        buf(64, 128),
        buf(64, 128),
        buf(128, 128),
        buf(128, 128),
        buf(128, 128),
        buf(128, 128),
        buf(128, 128),
        buf(128, 128),
        buf(128, 128),
        pltpu.VMEM((128, HW), F32),
        pltpu.VMEM((128, HW), F32),
        pltpu.VMEM((128, HW), F32),
        buf(128, HW),
        buf(128, HW),
        buf(128, D),
        buf(128, D),
        buf(128, D),
        buf(128, D),
        buf(64, D),
        dma((3, n_out)),
        dma((4,)),
        dma((2, n_out)),
        dma((2, n_out)),
        dma((n_out,)),
        dma((n_back,)),
        dma((n_back,)),
        dma((n_back,)),
        dma((12,)),
    ]
    parts = pl.pallas_call(
        kernel,
        out_shape=jax.ShapeDtypeStruct((4 * TOK, D), BF16),
        in_specs=[anywhere, anywhere, vmem, vmem, anywhere, anywhere, anywhere],
        out_specs=anywhere,
        scratch_shapes=scratch,
        compiler_params=pltpu.CompilerParams(
            collective_id=0, has_side_effects=True, vmem_limit_bytes=60 * 2**20
        ),
    )(layer_input, grad_output, expert_ids.T, route_weights.T, w_gate, w_up, w_down)
    return jnp.sum(parts.reshape(4, TOK, D).astype(F32), axis=0).astype(BF16)


def solution(mesh):
    both = ("node", "local")
    return jax.shard_map(
        local,
        mesh=mesh,
        in_specs=(
            P(both, None),
            P(both, None),
            P(both, None),
            P(both, None),
            P(both, None, None),
            P(both, None, None),
            P(both, None, None),
        ),
        out_specs=P(both, None),
        check_vma=False,
    )
```

```python
import jax
import jax.numpy as jnp
from jax import lax
from jax.experimental import pallas as pl
from jax.experimental.pallas import tpu as pltpu
from jax.sharding import PartitionSpec as P

MESH = pl.DeviceIdType.MESH
BF16 = jnp.bfloat16
F32 = jnp.float32

D = 3584
HW = 1024
TOK = 16
OUT_CUTS = (512, 768, 768, 768, 512, 256)
BACK_CUTS = (512,) * 7
HB = 1024
RB = 512
NB = 256


def pieces(cuts):
    starts = [sum(cuts[:i]) for i in range(len(cuts))]
    return tuple(zip(starts, cuts))


OUT_PIECES = pieces(OUT_CUTS)
BACK_PIECES = pieces(BACK_CUTS)


OUT_LAGS = (-3, 0, 1, 3)
BACK_LAGS = (0, 4, 7, 10)


def run_in_order(count, stages, lags, before):
    order = sorted((i + lag, k, i) for k, lag in enumerate(lags) for i in range(count))
    for _, k, i in order:
        if (i, k) in before:
            before[(i, k)]()
        stages[k](i)


def iota(shape, dim):
    return lax.broadcasted_iota(jnp.int32, shape, dim)


def dot(a, b):
    return jnp.dot(a, b, preferred_element_type=F32)


def dot_t(a, b):
    return lax.dot_general(a, b, (((1,), (1,)), ((), ())), preferred_element_type=F32)


def as01(mask):
    return jnp.where(mask, 1.0, 0.0).astype(BF16)


def rows(start, size):
    return pl.ds(pl.multiple_of(start, size), size)


def kernel(
    x_in,
    g_in,
    ids,
    route,
    wg_hbm,
    wu_hbm,
    wd_hbm,
    q_r,
    wg,
    wu,
    wd,
    w_tok,
    m1,
    m2,
    m_s,
    m_r,
    mx_s,
    mx_r,
    a1,
    a2,
    s1,
    s2,
    r1,
    r2,
    x_s,
    x_r,
    sel1,
    sel2,
    sel1t,
    sel2t,
    pick1,
    pick2,
    pick1t,
    pick2t,
    want1,
    want2,
    want_x,
    pre_gate,
    pre_up,
    hidden,
    d_gate,
    d_up,
    y_s,
    y_r,
    u_s,
    u_r,
    q_s,
    w_sem,
    meta_sem,
    h1_sem,
    h2_sem,
    x_sem,
    b1_sem,
    b2_sem,
    b3_sem,
    send_sem,
):
    node = lax.axis_index("node")
    xi = lax.axis_index("local")
    yi, zi, ci = node // 8, lax.rem(node // 2, 4), lax.rem(node, 2)

    def turn(v, k, size):
        return lax.rem(v + k, size)

    def device(y, z, c, x):
        return (y * 8 + z * 2 + c, x)

    far_first = (2, 1, 3)
    y_line = [(turn(yi, k, 4), device(turn(yi, k, 4), zi, ci, xi)) for k in far_first]
    z_line = [(turn(zi, k, 4), device(yi, turn(zi, k, 4), ci, xi)) for k in far_first]
    x_line = [(turn(xi, k, 4), device(yi, zi, ci, turn(xi, k, 4))) for k in far_first]
    steps = [(k, c) for k in far_first for c in (0, 1)] + [(0, 1)]
    zc_plane = [
        (turn(zi, k, 4) * 2 + turn(ci, c, 2), device(yi, turn(zi, k, 4), turn(ci, c, 2), xi))
        for k, c in steps
    ]
    yc_plane = [
        (turn(yi, k, 4) * 2 + turn(ci, c, 2), device(turn(yi, k, 4), zi, turn(ci, c, 2), xi))
        for k, c in steps
    ]
    lines = (y_line, z_line)
    planes = (zc_plane, yc_plane)
    line_at = (yi, zi)
    plane_at = (zi * 2 + ci, yi * 2 + ci)

    def local_copy(src, dst, sem):
        pltpu.make_async_copy(src, dst, sem).start()

    def remote_copy(src, dst, sem, send, target):
        pltpu.make_async_remote_copy(
            src_ref=src,
            dst_ref=dst,
            send_sem=send_sem.at[send],
            recv_sem=sem,
            device_id=target,
            device_id_type=MESH,
        ).start()

    def await_bytes(ref, sem):
        pltpu.make_async_copy(ref, ref, sem).wait()

    def weight_copies(i):
        start, width = OUT_PIECES[i]
        cut = pl.ds(start, width)
        return (
            pltpu.make_async_copy(wg_hbm.at[0, cut, :], wg.at[cut, :], w_sem.at[0, i]),
            pltpu.make_async_copy(wu_hbm.at[0, cut, :], wu.at[cut, :], w_sem.at[1, i]),
            pltpu.make_async_copy(wd_hbm.at[0, :, cut], wd.at[:, cut], w_sem.at[2, i]),
        )

    barrier = pltpu.get_barrier_semaphore()
    pairs = zip(zc_plane[:-1], yc_plane[:-1])
    partners = [d for pair in pairs for _, d in pair] + [zc_plane[-1][1]]
    partners = [x_line[0][1]] + partners + [d for _, d in x_line[1:]]
    for target in partners:
        pl.semaphore_signal(barrier, inc=1, device_id=target, device_id_type=MESH)

    for i in range(len(OUT_PIECES)):
        for copy in weight_copies(i):
            copy.start()

    down = iota((128, TOK), 0)
    table_t = jnp.zeros((128, TOK), F32)
    id_block, route_block = ids[...], route[...].astype(F32)
    for k in range(8):
        table_t += jnp.where(id_block[k : k + 1, :] == down, route_block[k : k + 1, :], 0.0)
    small0, small1 = iota((TOK, TOK), 0), iota((TOK, TOK), 1)
    table = dot_t(as01(small0 == small1), table_t.astype(BF16))
    row, col = iota((128, 128), 0), iota((128, 128), 1)
    in_group = dot(as01(table > 0), as01((row >> 2) == (col >> 2))) > 0.5
    rank = dot(as01(small1 < small0), as01(in_group))
    w_tok[:, 0:128] = table.astype(BF16)
    w_tok[:, 128:256] = jnp.where(in_group, rank + 1.0, 0.0).astype(BF16)
    first = (col & 3) == 0
    group = col >> 2
    place = row >> 4
    want1[...] = as01(first & ((group >> 3) == yi) & ((group & 7) == place))
    want2[...] = as01(
        first & (((group >> 1) & 3) == zi) & (((group >> 3) * 2 + (group & 1)) == place)
    )
    want_x[...] = as01(col == node * 4 + (row >> 5))

    pl.semaphore_wait(barrier, len(partners))

    metas = (m1, m2)
    gathered = (a1, a2)
    sources = (x_in, g_in)
    spread_s, spread_r = (s1, s2), (r1, r2)
    sel, sel_t = (sel1, sel2), (sel1t, sel2t)
    pick, pick_t = (pick1, pick2), (pick1t, pick2t)
    wants = (want1, want2)

    for p in (0, 1):
        mine = metas[p].at[rows(line_at[p] * TOK, TOK), :]
        for _, target in lines[p]:
            remote_copy(w_tok, mine, meta_sem.at[p], p, target)
        local_copy(w_tok, mine, meta_sem.at[p])

    def gather(i):
        start, width = OUT_PIECES[i]
        cut = pl.ds(start, width)
        for p in (0, 1):
            mine = gathered[p].at[rows(line_at[p] * TOK, TOK), cut]
            for _, target in lines[p]:
                remote_copy(sources[p].at[:, cut], mine, h1_sem.at[p, i], 4 + p, target)
            local_copy(sources[p].at[:, cut], mine, h1_sem.at[p, i])

    def spread(i):
        start, width = OUT_PIECES[i]
        cut = pl.ds(start, width)
        for p in (0, 1):
            await_bytes(gathered[p].at[:, cut], h1_sem.at[p, i])
            spread_s[p][:, cut] = dot(sel[p][...], gathered[p][:, cut]).astype(BF16)
            mine = rows(plane_at[p] * TOK, TOK)
            for at, target in planes[p]:
                remote_copy(
                    spread_s[p].at[rows(at * TOK, TOK), cut],
                    spread_r[p].at[mine, cut],
                    h2_sem.at[p, i],
                    6 + p,
                    target,
                )
            local_copy(spread_s[p].at[mine, cut], spread_r[p].at[mine, cut], h2_sem.at[p, i])

    def forward(i):
        start, width = OUT_PIECES[i]
        cut = pl.ds(start, width)
        for p in (0, 1):
            await_bytes(spread_r[p].at[:, cut], h2_sem.at[p, i])
            x_s[:, pl.ds(2 * start + p * width, width)] = dot(
                pick[p][...], spread_r[p][:, cut]
            ).astype(BF16)
        both = pl.ds(2 * start, 2 * width)
        mine = rows(xi * 32, 32)
        for at, target in x_line:
            remote_copy(x_s.at[rows(at * 32, 32), both], x_r.at[mine, both], x_sem.at[i], 8, target)
        local_copy(x_s.at[mine, both], x_r.at[mine, both], x_sem.at[i])

    def multiply(i):
        start, width = OUT_PIECES[i]
        cut = pl.ds(start, width)
        both = pl.ds(2 * start, 2 * width)
        for copy in weight_copies(i):
            copy.wait()
        await_bytes(x_r.at[:, both], x_sem.at[i])
        x_part = x_r[:, pl.ds(2 * start, width)]
        g_part = x_r[:, pl.ds(2 * start + width, width)]

        @pl.loop(0, HW // HB)
        def _(n):
            block = rows(n * HB, HB)
            gate = dot(x_part, wg[cut, block])
            up = dot(x_part, wu[cut, block])
            hid = dot_t(g_part, wd[block, cut])
            if i == 0:
                pre_gate[:, block] = gate
                pre_up[:, block] = up
                hidden[:, block] = hid
            else:
                pre_gate[:, block] += gate
                pre_up[:, block] += up
                hidden[:, block] += hid

    def choose_tokens():
        r0, c0 = iota((128, 64), 0), iota((128, 64), 1)
        fits = ((r0 >> 2) & 3) == (c0 >> 4)
        slot = ((r0 & 3) + 1).astype(F32)
        for p in (0, 1):
            await_bytes(metas[p], meta_sem.at[p])
        for p in (0, 1):
            found = dot_t(wants[p][...], metas[p][:, 128:256])
            sel[p][...] = as01(fits & (found == slot))
        m_s[...] = dot(sel1[...], m1[:, 0:128]).astype(BF16)
        mine = rows(plane_at[0] * TOK, TOK)
        for at, target in planes[0]:
            remote_copy(m_s.at[rows(at * TOK, TOK), :], m_r.at[mine, :], meta_sem.at[2], 2, target)
        local_copy(m_s.at[mine, :], m_r.at[mine, :], meta_sem.at[2])

    def choose_slots():
        row, col = iota((128, 128), 0), iota((128, 128), 1)
        await_bytes(m_r, meta_sem.at[2])
        hits = as01(m_r[...].astype(F32) > 0)
        hit = dot_t(want_x[...], hits) > 0.5
        rank = dot(as01(hit), as01(row < col)).astype(jnp.int32)
        p1 = as01(hit & (rank == (row & 31)))
        pick1[...] = p1
        pick2[...] = dot(p1, as01(swapped(row) == col)).astype(BF16)

    def swapped(slot):
        return ((slot >> 2) & 3) * 32 + (slot & 16) + (slot >> 5) * 4 + (slot & 3)

    def choose_late():
        mx_s[...] = dot(pick1[...], m_r[...]).astype(BF16)
        mine = rows(xi * 32, 32)
        for at, target in x_line:
            remote_copy(mx_s.at[rows(at * 32, 32), :], mx_r.at[mine, :], meta_sem.at[3], 3, target)
        local_copy(mx_s.at[mine, :], mx_r.at[mine, :], meta_sem.at[3])
        row, col = iota((128, 128), 0), iota((128, 128), 1)
        same = as01(row == col)
        p1t = dot_t(same, pick1[...]).astype(BF16)
        pick1t[...] = p1t
        pick2t[...] = dot(as01(swapped(row) == col), p1t).astype(BF16)
        for p in (0, 1):
            sel_t[p][...] = dot_t(same[0:64, 0:64], sel[p][...]).astype(BF16)

    def activate():
        await_bytes(mx_r, meta_sem.at[3])
        scale = jnp.sum(
            jnp.where(iota((128, 128), 1) == node * 4 + xi, mx_r[...].astype(F32), 0.0),
            axis=1,
            keepdims=True,
        )

        @pl.loop(0, HW // NB)
        def _(n):
            block = rows(n * NB, NB)
            gate, up = pre_gate[:, block], pre_up[:, block]
            grad = scale * hidden[:, block]
            s = jax.nn.sigmoid(gate)
            d_gate[:, block] = (grad * up * s * (1.0 + gate * (1.0 - s))).astype(BF16)
            d_up[:, block] = (grad * gate * s).astype(BF16)

    def back_rows(i):
        start, width = BACK_PIECES[i]
        cut = pl.ds(start, width)

        @pl.loop(0, width // RB)
        def _(n):
            block = rows(start + n * RB, RB)
            total = dot_t(d_gate[...], wg[block, :]) + dot_t(d_up[...], wu[block, :])
            y_s[:, block] = total.astype(BF16)

        mine = rows(xi * 32, 32)
        for at, target in x_line:
            remote_copy(y_s.at[rows(at * 32, 32), cut], y_r.at[mine, cut], b1_sem.at[i], 9, target)
        local_copy(y_s.at[mine, cut], y_r.at[mine, cut], b1_sem.at[i])

    def back_slots(i):
        start, width = BACK_PIECES[i]
        cut = pl.ds(start, width)
        p = i % 2
        await_bytes(y_r.at[:, cut], b1_sem.at[i])
        u_s[:, cut] = dot(pick_t[p][...], y_r[:, cut]).astype(BF16)
        mine = rows(plane_at[p] * TOK, TOK)
        for at, target in planes[p]:
            remote_copy(
                u_s.at[rows(at * TOK, TOK), cut], u_r.at[mine, cut], b2_sem.at[i], 10, target
            )
        local_copy(u_s.at[mine, cut], u_r.at[mine, cut], b2_sem.at[i])

    def back_tokens(i):
        start, width = BACK_PIECES[i]
        cut = pl.ds(start, width)
        p = i % 2
        await_bytes(u_r.at[:, cut], b2_sem.at[i])
        q_s[:, cut] = dot(sel_t[p][...], u_r[:, cut]).astype(BF16)
        mine = rows(line_at[p] * TOK, TOK)
        for at, target in lines[p]:
            remote_copy(
                q_s.at[rows(at * TOK, TOK), cut], q_r.at[mine, cut], b3_sem.at[i], 11, target
            )
        local_copy(q_s.at[mine, cut], q_r.at[mine, cut], b3_sem.at[i])

    def finish(i):
        start, width = BACK_PIECES[i]
        await_bytes(q_r.at[:, pl.ds(start, width)], b3_sem.at[i])

    out_extra = {
        (0, 1): choose_tokens,
        (0, 2): choose_slots,
        (0, 3): choose_late,
    }
    run_in_order(len(OUT_PIECES), (gather, spread, forward, multiply), OUT_LAGS, out_extra)
    activate()
    run_in_order(len(BACK_PIECES), (back_rows, back_slots, back_tokens, finish), BACK_LAGS, {})

    for p in (0, 1):
        await_bytes(metas[p].at[0:48, :], send_sem.at[p])
        await_bytes(gathered[p].at[0:48, :], send_sem.at[4 + p])
        await_bytes(spread_s[p].at[0:112, :], send_sem.at[6 + p])
    await_bytes(m_s.at[0:112, :], send_sem.at[2])
    await_bytes(mx_s.at[0:96, :], send_sem.at[3])
    await_bytes(x_s.at[0:96, :], send_sem.at[8])
    await_bytes(y_s.at[0:96, :], send_sem.at[9])
    await_bytes(u_s.at[0:112, :], send_sem.at[10])
    await_bytes(q_s.at[0:48, :], send_sem.at[11])


def local(layer_input, grad_output, expert_ids, route_weights, w_gate, w_up, w_down):
    vmem = pl.BlockSpec(memory_space=pltpu.VMEM)
    anywhere = pl.BlockSpec(memory_space=pl.ANY)
    dma = pltpu.SemaphoreType.DMA
    n_out, n_back = len(OUT_PIECES), len(BACK_PIECES)

    def buf(*shape):
        return pltpu.VMEM(shape, BF16)

    scratch = [
        buf(D, HW),
        buf(D, HW),
        buf(HW, D),
        buf(TOK, 256),
        buf(64, 256),
        buf(64, 256),
        buf(128, 128),
        buf(128, 128),
        buf(128, 128),
        buf(128, 128),
        buf(64, D),
        buf(64, D),
        buf(128, D),
        buf(128, D),
        buf(128, D),
        buf(128, D),
        buf(128, 2 * D),
        buf(128, 2 * D),
        buf(128, 64),
        buf(128, 64),
        buf(64, 128),
        buf(64, 128),
        buf(128, 128),
        buf(128, 128),
        buf(128, 128),
        buf(128, 128),
        buf(128, 128),
        buf(128, 128),
        buf(128, 128),
        pltpu.VMEM((128, HW), F32),
        pltpu.VMEM((128, HW), F32),
        pltpu.VMEM((128, HW), F32),
        buf(128, HW),
        buf(128, HW),
        buf(128, D),
        buf(128, D),
        buf(128, D),
        buf(128, D),
        buf(64, D),
        dma((3, n_out)),
        dma((4,)),
        dma((2, n_out)),
        dma((2, n_out)),
        dma((n_out,)),
        dma((n_back,)),
        dma((n_back,)),
        dma((n_back,)),
        dma((12,)),
    ]
    parts = pl.pallas_call(
        kernel,
        out_shape=jax.ShapeDtypeStruct((4 * TOK, D), BF16),
        in_specs=[anywhere, anywhere, vmem, vmem, anywhere, anywhere, anywhere],
        out_specs=anywhere,
        scratch_shapes=scratch,
        compiler_params=pltpu.CompilerParams(
            collective_id=0, has_side_effects=True, vmem_limit_bytes=60 * 2**20
        ),
    )(layer_input, grad_output, expert_ids.T, route_weights.T, w_gate, w_up, w_down)
    return jnp.sum(parts.reshape(4, TOK, D).astype(F32), axis=0).astype(BF16)


def solution(mesh):
    both = ("node", "local")
    return jax.shard_map(
        local,
        mesh=mesh,
        in_specs=(
            P(both, None),
            P(both, None),
            P(both, None),
            P(both, None),
            P(both, None, None),
            P(both, None, None),
            P(both, None, None),
        ),
        out_specs=P(both, None),
        check_vma=False,
    )
```
